128 devices in a mesh: sect: 4 (over y_lo, core), tile: 32 (over x, y_hi, z).
Axes of the slice: x: 4, y: 4 (y_hi: 2, y_lo: 2; y = y_hi * 2 + y_lo), z: 4, core: 2. Of those that a mesh axis runs over, the one named last changes fastest.
Arguments:
- tracer_values: float32 [4, 16, 512, 3584], P('sect', None, 'tile'), may hold values from -6 to 6
- courant_numbers: bfloat16 [2, 4, 16, 512, 3584], P(None, 'sect', None, 'tile'), may hold values from -0.29882812 to 0.29882812
- diffusion_numbers: bfloat16 [4, 16, 512, 3584], P('sect', None, 'tile'), may hold values from 0.049804688 to 0.19921875
- water_indicator: int32 [512, 3584], P('tile'), may hold values 0 or 1
- downward_lane_pairs: int32 [4, 32, 2, 32, 4], P('sect', 'tile'), may hold values from 0 to 447
- downward_lane_number: int32 [4, 32, 32], P('sect', 'tile'), may hold values from 0 to 4, as said below
- downward_patch_matrix: bfloat16 [4, 32, 32, 4, 128, 128], P('sect', 'tile'), may hold values from -0.5 to 0.5
- upward_lane_pairs: int32 [4, 32, 2, 32, 4], P('sect', 'tile'), may hold values from 0 to 447
- upward_lane_number: int32 [4, 32, 32], P('sect', 'tile'), may hold values from 0 to 4, as said below
- upward_patch_matrix: bfloat16 [4, 32, 32, 4, 128, 128], P('sect', 'tile'), may hold values from -0.5 to 0.5
Outputs:
- advanced: float32 [4, 16, 512, 3584], P('sect', None, 'tile')
The draws below stay inside these ranges and needn't reach their ends.
Inputs may be any that keep to these rules, and one draw needn't show every extreme that they name: `downward_lane_number`: zero on section 3; in every draw one ocean tile has 4 live slots from every atmosphere device. `upward_lane_number`: zero on section 3; in every draw one ocean tile fills 4 slots of every atmosphere device.
All inputs are finite; a program needn't handle non-finite values. No bound on the sum of `water_indicator` on one device may be relied on, other than what follows from the above.
Results may differ from the reference program's by a relative error of at most 0.00032.
Values may be sent and summed in bfloat16 or wider, within the bound.
A program may use at most 128 MiB of HBM per device.

```python
import math
import jax
import jax.numpy as jnp
from jax import lax

LEV = 16
RX = 3584
PATCH_POINTS = 128
LANE_LIMIT = 4
SUBSTEPS = 3
NY = 512
PATCHES_EACH_CHIP = 448
N_SECT = 4
N_TILE = 32


def section_counts(key):
    counts = jax.random.randint(key, (N_SECT, N_TILE, N_TILE), 0, LANE_LIMIT + 1)
    chosen = jax.random.randint(jax.random.fold_in(key, 5), (), 0, N_TILE)
    target_tile = jnp.arange(N_TILE)[None, None, :]
    counts = jnp.where(target_tile == chosen, LANE_LIMIT, counts)
    sect_ids = jnp.arange(N_SECT)[:, None, None]
    return jnp.where(sect_ids == N_SECT - 1, 0, counts).astype(jnp.int32)


def draw_downward_lane_number(key, part):
    key = jax.random.fold_in(key, 11)
    return section_counts(key)


def draw_upward_lane_number(key, part):
    key = jax.random.fold_in(key, 12)
    return section_counts(key)


def set_ends(drawn, own_key, low, high):
    longest = drawn.shape.index(max(drawn.shape))
    spots = []
    for shift in (0, 1):
        where = [jax.random.randint(jax.random.fold_in(own_key, axis), (), 0, length) for axis, length in enumerate(drawn.shape)]
        where[longest] = (where[longest] + shift) % drawn.shape[longest]
        spots.append(tuple(where))
    return drawn.at[spots[0]].set(low).at[spots[1]].set(high)


def block_scale(rng, shape, shards, least, largest):
    loudness = 1.0
    for position, blocks in shards:
        draws = jax.random.uniform(jax.random.fold_in(jax.random.fold_in(rng, 6), position), (blocks,), jnp.float32, least / len(shards), largest / len(shards))
        loudness = loudness * jnp.repeat(jnp.exp(draws), shape[position] // blocks).reshape((-1,) + (1,) * (len(shape) - 1 - position))
    return loudness


def centred(key, extent, spread, most, split=(), kind=jnp.bfloat16):
    drawn = spread * jax.random.normal(key, extent, jnp.float32)
    if split:
        drawn = drawn * block_scale(key, extent, split, -0.22, 0.18)
    return jnp.clip(drawn, -most, most).astype(kind)


def setup_inputs(seed: int = 0) -> dict:
    streams_of = jax.random.split(jax.random.key(seed), 11)
    tracer_values = centred(streams_of[0], (N_SECT, LEV, NY, RX), 1.0, 6.0, ((0, 4), (2, 32)), jnp.float32)
    courant_numbers = jnp.clip(jax.random.uniform(streams_of[1], (2, N_SECT, LEV, NY, RX), jnp.float32, -0.29882812, 0.29882812) * block_scale(streams_of[1], (2, N_SECT, LEV, NY, RX), ((1, 4), (3, 32)), -0.4, 0.0), -0.29882812, 0.29882812).astype(jnp.bfloat16)
    diffusion_numbers = jnp.clip(jnp.exp(math.log(0.19921875) - 1.3862944 * jax.random.uniform(streams_of[2], (N_SECT, LEV, NY, RX), jnp.float32) ** block_scale(streams_of[2], (N_SECT, LEV, NY, RX), ((0, 4), (2, 32)), -0.2, 0.2)), 0.049804688, 0.19921875).astype(jnp.bfloat16)
    water_indicator = set_ends((jax.random.randint(streams_of[3], (NY, RX), 0, 10) < 7).astype(jnp.int32), jax.random.fold_in(streams_of[3], 1), 0, 1)
    downward_lane_pairs = set_ends(jax.random.randint(streams_of[4], (N_SECT, N_TILE, 2, N_TILE, LANE_LIMIT), 0, PATCHES_EACH_CHIP), jax.random.fold_in(streams_of[4], 1), 0, PATCHES_EACH_CHIP - 1).astype(jnp.int32)
    downward_lane_number = draw_downward_lane_number(jax.random.fold_in(streams_of[10], 71), 0)
    downward_patch_matrix = centred(streams_of[6], (N_SECT, N_TILE, N_TILE, LANE_LIMIT, PATCH_POINTS, PATCH_POINTS), PATCH_POINTS ** -0.5, 0.5, ((0, 4), (1, 32)))
    upward_lane_pairs = set_ends(jax.random.randint(streams_of[7], (N_SECT, N_TILE, 2, N_TILE, LANE_LIMIT), 0, PATCHES_EACH_CHIP), jax.random.fold_in(streams_of[7], 1), 0, PATCHES_EACH_CHIP - 1).astype(jnp.int32)
    upward_lane_number = draw_upward_lane_number(jax.random.fold_in(streams_of[10], 71), 0)
    upward_patch_matrix = centred(streams_of[9], (N_SECT, N_TILE, N_TILE, LANE_LIMIT, PATCH_POINTS, PATCH_POINTS), PATCH_POINTS ** -0.5, 0.5, ((0, 4), (1, 32)))
    return dict(tracer_values=tracer_values, courant_numbers=courant_numbers, diffusion_numbers=diffusion_numbers, water_indicator=water_indicator, downward_lane_pairs=downward_lane_pairs, downward_lane_number=downward_lane_number, downward_patch_matrix=downward_patch_matrix, upward_lane_pairs=upward_lane_pairs, upward_lane_number=upward_lane_number, upward_patch_matrix=upward_patch_matrix)


def stencil(padded, wind_east, wind_north, mixing_now, wet_mask):
    centre = padded[..., 1:-1, :]
    upper_row = padded[..., :-2, :]
    lower_row = padded[..., 2:, :]
    widened = jnp.pad(centre, [(0, 0)] * (centre.ndim - 1) + [(1, 1)])
    right_col = widened[..., 2:]
    left_col = widened[..., :-2]
    updated = (centre - 0.5 * wind_east * (right_col - left_col) - 0.5 * wind_north * (lower_row - upper_row)
               + mixing_now * (right_col + left_col + upper_row + lower_row - 4.0 * centre))
    return updated * wet_mask


def patch_scaled_terms(pair):
    return jnp.einsum("tdci,tdcij->tdcj", pair[0].astype(jnp.float32), pair[1].astype(jnp.float32))


def reference(tracer_values, courant_numbers, diffusion_numbers, water_indicator, downward_lane_pairs, downward_lane_number, downward_patch_matrix, upward_lane_pairs, upward_lane_number, upward_patch_matrix):
    water_indicator_real = water_indicator.astype(jnp.float32)
    bottom = tracer_values[:, 0].astype(jnp.bfloat16).reshape(N_SECT, N_TILE, PATCHES_EACH_CHIP, PATCH_POINTS)
    sect_ix = jnp.arange(N_SECT, dtype=jnp.int32)[:, None, None, None]
    tile_ix = jnp.arange(N_TILE, dtype=jnp.int32)[None, :, None, None]
    dest_ix = jnp.arange(N_TILE, dtype=jnp.int32)[None, None, :, None]
    lane_ordinal = jnp.arange(LANE_LIMIT, dtype=jnp.int32)[None, None, None, :]
    shape_four = (N_SECT, N_TILE, N_TILE, LANE_LIMIT)
    partition_patch = jnp.broadcast_to(sect_ix, shape_four)
    panel_patch = jnp.broadcast_to(tile_ix, shape_four)
    target_patch = jnp.broadcast_to(dest_ix, shape_four)
    selected_blocks = bottom[partition_patch, panel_patch, downward_lane_pairs[:, :, 0]]
    products = lax.map(patch_scaled_terms, (selected_blocks, downward_patch_matrix))
    active = lane_ordinal < downward_lane_number[..., None]
    products = jnp.where(active[..., None], products, 0.0).astype(jnp.bfloat16)
    flux_blocks = jnp.zeros((N_TILE, PATCHES_EACH_CHIP, PATCH_POINTS), jnp.float32).at[target_patch, downward_lane_pairs[:, :, 1]].add(products.astype(jnp.float32))
    flux_field = flux_blocks.reshape(NY, RX)
    seabed_tracer = tracer_values[N_SECT - 1, 0] + flux_field * water_indicator_real
    skin_heat_field = (seabed_tracer * water_indicator_real).astype(jnp.bfloat16).reshape(N_TILE, PATCHES_EACH_CHIP, PATCH_POINTS)
    collected_patches = skin_heat_field[target_patch, upward_lane_pairs[:, :, 0]]
    incoming_patches = lax.map(patch_scaled_terms, (collected_patches, upward_patch_matrix))
    upward_lane_live = lane_ordinal < upward_lane_number[..., None]
    incoming_patches = jnp.where(upward_lane_live[..., None], incoming_patches, 0.0)
    air_patch_lines = jnp.zeros((N_SECT, N_TILE, PATCHES_EACH_CHIP, PATCH_POINTS), jnp.float32).at[partition_patch, panel_patch, upward_lane_pairs[:, :, 1]].add(incoming_patches)
    atm_field = air_patch_lines.reshape(N_SECT, NY, RX)
    ocean_flag = (jnp.arange(N_SECT) == N_SECT - 1).astype(jnp.float32)[:, None, None]
    bottom_new = tracer_values[:, 0] + 0.5 * atm_field + ocean_flag * flux_field[None] * water_indicator_real[None]
    field = tracer_values.at[:, 0].set(bottom_new)
    wet_mask = (ocean_flag * water_indicator_real[None] + (1.0 - ocean_flag))[:, None]
    wind_east = courant_numbers[0].astype(jnp.float32)
    wind_north = courant_numbers[1].astype(jnp.float32)
    mixing_now = diffusion_numbers.astype(jnp.float32)
    for substep in range(SUBSTEPS):
        padded = jnp.pad(field, ((0, 0), (0, 0), (1, 1), (0, 0)))
        field = stencil(padded, wind_east, wind_north, mixing_now, wet_mask)
    return field
```

```python
import functools

import jax
import jax.numpy as jnp
from jax import lax
from jax.experimental import pallas as pl
from jax.experimental.pallas import tpu as pltpu
from jax.sharding import PartitionSpec as P

F32 = jnp.float32
BF16 = jnp.bfloat16
MESH = pl.DeviceIdType.MESH
LANES = 128
SUBSTEPS = 3
CODE = 1024


def shifted_rows(upper, lower, north, south):
    row = lax.broadcasted_iota(jnp.int32, upper.shape, 0)
    upper_down = pltpu.roll(upper, 1, 0)
    lower_down = pltpu.roll(lower, 1, 0)
    upper_up = pltpu.roll(upper, 7, 0)
    lower_up = pltpu.roll(lower, 7, 0)
    return (
        jnp.where(row == 0, north, upper_down),
        jnp.where(row == 0, upper_down, lower_down),
        jnp.where(row == 7, lower_up, upper_up),
        jnp.where(row == 7, south, lower_up),
    )


def column_chunks(width, tiles):
    step = tiles * LANES
    return [(start, step) for start in range(0, width, step)]


def shifted_columns(x, before, after):
    size = x.shape[1]
    lane = lax.broadcasted_iota(jnp.int32, before.shape, 1)
    east = pltpu.roll(x, size - 1, 1)
    west = pltpu.roll(x, 1, 1)
    east_end = jnp.where(lane == LANES - 1, pltpu.roll(after, LANES - 1, 1), east[:, size - LANES :])
    west_end = jnp.where(lane == 0, pltpu.roll(before, 1, 1), west[:, :LANES])
    return (
        jnp.concatenate([east[:, : size - LANES], east_end], axis=1),
        jnp.concatenate([west_end, west[:, LANES:]], axis=1),
    )


def substep_level(src, dst, coef, halo_rows, level, keep):
    columns = src.shape[-1]
    north = halo_rows[0, pl.ds(level, 1), :]
    south = halo_rows[1, pl.ds(level, 1), :]
    for start, size in column_chunks(columns, 7):
        cols = pl.ds(start, size)
        upper = src[level, 0:8, cols]
        lower = src[level, 8:16, cols]
        upper_n, lower_n, upper_s, lower_s = shifted_rows(
            upper, lower, north[:, start : start + size], south[:, start : start + size]
        )
        before = pl.ds((start - LANES) % columns, LANES)
        after = pl.ds((start + size) % columns, LANES)
        results = []
        for x, xn, xs, row in ((upper, upper_n, upper_s, 0), (lower, lower_n, lower_s, 8)):
            rows = pl.ds(row, 8)
            east, west = shifted_columns(x, src[level, rows, before], src[level, rows, after])
            new = (
                coef[0, level, rows, cols] * x
                + coef[1, level, rows, cols] * east
                + coef[2, level, rows, cols] * west
                + coef[3, level, rows, cols] * xn
                + coef[4, level, rows, cols] * xs
            )
            dst[level, rows, cols] = new
            results.append(new)
        if keep is not None:
            keep(results[0], results[1], start, size)


def over_levels(first, count, act, unroll=4):
    def some(i, carry):
        for j in range(unroll):
            act(first + i * unroll + j)
        return carry

    lax.fori_loop(0, count // unroll, some, 0)
    for level in range(first + count // unroll * unroll, first + count):
        act(level)


def coefficients(u, v, k, wet, first, last):
    u = 0.5 * u
    v = 0.5 * v
    east = k - u
    west = k + u
    col = lax.broadcasted_iota(jnp.int32, u.shape, 1)
    if first is not None:
        west = jnp.where(col == first, 0.0, west)
    if last is not None:
        east = jnp.where(col == last, 0.0, east)
    parts = (1.0 - 4.0 * k, east, west, k + v, k - v)
    return parts if wet is None else [wet * c for c in parts]


def kernel_body(
    sections,
    tiles,
    tracer,
    courant,
    diffusion,
    water,
    down_pairs,
    down_number,
    down_matrix,
    up_pairs,
    up_number,
    up_matrix,
    field_b,
    field_a,
    winds,
    mixing,
    coef,
    mask_int,
    wet_mask,
    pairs_d,
    number_d,
    matrix_d,
    pairs_u,
    number_u,
    matrix_u,
    down_send,
    down_recv,
    up_send,
    up_recv,
    lhs_all,
    onehot_up,
    sst,
    halo_stage,
    halo_rows,
    halo_send,
    halo_recv,
    scale_send,
    scale_recv,
    edge_send,
    edge_recv,
    side_send,
    side_recv,
    zero_a,
    zero_b,
    coef_zero,
    load_sem,
    remap_sem,
    halo_sems,
    scale_sems,
    edge_sems,
    side_sems,
):
    sect = lax.axis_index("sect")
    tile = lax.axis_index("tile")
    ocean_sect = sections - 1
    is_ocean = sect == ocean_sect
    is_atm = sect != ocean_sect
    has_north = tile > 0
    has_south = tile < tiles - 1
    levels, rows, columns = field_a.shape
    col_tiles = columns // LANES
    blocks = rows * col_tiles
    blocks_pad = 512
    lanes_i = functools.partial(lax.broadcasted_iota, jnp.int32)

    def load(src, dst, number):
        return pltpu.make_async_copy(src, dst, load_sem.at[number])

    loads = [
        load(tracer.at[pl.ds(0, 1)], field_a.at[pl.ds(0, 1)], 0),
        load(down_pairs, pairs_d, 1),
        load(down_number, number_d, 2),
        load(up_pairs, pairs_u, 3),
        load(up_number, number_u, 4),
        load(down_matrix, matrix_d, 5),
        load(tracer.at[pl.ds(1, levels - 1)], field_a.at[pl.ds(1, levels - 1)], 6),
        load(water, mask_int, 7),
        load(courant, winds, 8),
        load(diffusion, mixing, 9),
        load(up_matrix, matrix_u, 10),
    ]
    for copy in loads:
        copy.start()

    barrier = pltpu.get_barrier_semaphore()

    def greet(device):
        pl.semaphore_signal(barrier, inc=1, device_id=device, device_id_type=MESH)

    @pl.when(is_atm)
    def _():
        def one(i, carry):
            greet((ocean_sect, lax.rem(tile + i, tiles)))
            return carry

        lax.fori_loop(0, tiles, one, 0)

    @pl.when(is_ocean)
    def _():
        def one(i, carry):
            for s in range(ocean_sect):
                greet((s, lax.rem(tile + i, tiles)))
            return carry

        lax.fori_loop(0, tiles, one, 0)

    @pl.when(has_north)
    def _():
        greet((sect, tile - 1))

    @pl.when(has_south)
    def _():
        greet((sect, tile + 1))

    for edge, number in ((has_north, 0), (has_south, 1)):

        @pl.when(jnp.logical_not(edge))
        def _(number=number):
            for step in range(SUBSTEPS):
                halo_recv[step, number] = jnp.zeros(halo_recv.shape[2:], halo_recv.dtype)
                scale_recv[step, number] = jnp.zeros(scale_recv.shape[2:], F32)
            edge_recv[number] = jnp.zeros(edge_recv.shape[1:], F32)
            side_recv[number] = jnp.zeros(side_recv.shape[1:], BF16)

    for number in (1, 2, 3, 4):
        loads[number].wait()

    slots = pairs_d.shape[1]
    eye = lanes_i((tiles, tiles), 0) == lanes_i((tiles, tiles), 1)

    def ids_by_tile(pairs_ref, number_ref, which, targets):
        ids = pairs_ref[which].astype(F32)
        if targets:
            live = lanes_i((slots, tiles), 0) < number_ref[...]
            ids = jnp.where(live, ids + 1.0, 0.0)
        return [jnp.sum(jnp.where(eye, ids[c : c + 1], 0.0), axis=1, keepdims=True) for c in range(slots)]

    down_src = [ids + 1.0 for ids in ids_by_tile(pairs_d, number_d, 0, False)]
    down_dst = ids_by_tile(pairs_d, number_d, 1, True)
    up_src = ids_by_tile(pairs_u, number_u, 0, False)
    up_dst = ids_by_tile(pairs_u, number_u, 1, True)
    lane = lanes_i((tiles, LANES), 1)

    def block_of(index):
        return (index % rows) * col_tiles + index // rows

    place = lax.rem(tile, 16) * 8
    target_row = jnp.zeros((tiles, LANES), F32)
    for c in range(slots):
        target_row = jnp.where(lane == place + c, down_dst[c], target_row)
    for c in range(slots):
        ids = jnp.broadcast_to(up_src[c], (tiles, LANES))
        if c == 0:
            ids = ids + CODE * target_row
        down_send[:, 4 + c, :] = ids

    def row_of_ids(ids, first, count):
        dest = lanes_i((count, 8 * count), 0)
        at = lanes_i((count, 8 * count), 1)
        spread = jnp.zeros((count, 8 * count), F32)
        for c in range(slots):
            spread = jnp.where(at == 8 * dest + c, ids[c][first : first + count], spread)
        return jnp.sum(spread, axis=0, keepdims=True)

    @pl.when(is_atm)
    def _():
        place_block = (block_of(lanes_i((blocks, LANES), 0)) + 1).astype(F32)
        for half in range(tiles // 16):
            ids = pltpu.roll(row_of_ids(up_dst, 16 * half, 16), 4, 1)
            onehot_up[:, half * LANES : (half + 1) * LANES] = jnp.where(place_block == ids, 1.0, 0.0).astype(BF16)

    loads[0].wait()

    @pl.when(is_atm)
    def _():
        for k in range(col_tiles):
            sst[k * rows : (k + 1) * rows, :] = field_a[0, :, k * LANES : (k + 1) * LANES].astype(BF16)
        sst[blocks:blocks_pad, :] = jnp.zeros((blocks_pad - blocks, LANES), BF16)
        place_block = (block_of(lanes_i((blocks_pad, LANES), 0)) + 1).astype(F32)
        for half in range(tiles // 16):
            ids = row_of_ids(down_src, 16 * half, 16)
            onehot = jnp.where(place_block == ids, 1.0, 0.0).astype(BF16)
            picked = lax.dot_general(onehot, sst[...], (((0,), (0,)), ((), ())), preferred_element_type=F32)
            lhs_all[half * 16 : (half + 1) * 16] = picked.reshape(16, 8, LANES)

    def remap(rows_ref, matrix_ref, first, tile_index):
        x = rows_ref[tile_index]
        sub = lanes_i((8, LANES), 0)
        lhs = jnp.concatenate([jnp.where(sub == first + c, x, 0.0) for c in range(slots)], axis=1).astype(BF16)
        matrix = matrix_ref[tile_index].reshape(slots * LANES, LANES)
        return jnp.dot(lhs, matrix, preferred_element_type=F32)

    loads[5].wait()

    @pl.when(is_atm)
    def _():
        def some(i, carry):
            for j in range(8):
                d = i * 8 + j
                product = remap(lhs_all, matrix_d, 0, d).astype(BF16).astype(F32)
                down_send[d, 0:4, :] = product[0:4]
            return carry

        lax.fori_loop(0, tiles // 8, some, 0)

    pl.semaphore_wait(
        barrier,
        jnp.where(is_atm, tiles, ocean_sect * tiles) + has_north.astype(jnp.int32) + has_south.astype(jnp.int32),
    )

    @pl.when(is_atm)
    def _():
        def one(i, carry):
            d = lax.rem(tile + i, tiles)
            pltpu.make_async_remote_copy(
                src_ref=down_send.at[d],
                dst_ref=down_recv.at[sect * tiles + tile],
                send_sem=remap_sem.at[0],
                recv_sem=remap_sem.at[1],
                device_id=(ocean_sect, d),
                device_id_type=MESH,
            ).start()
            return carry

        lax.fori_loop(0, tiles, one, 0)

    def neighbour_copy(send, recv, sems, number):
        to = (sect, tile + 1) if number == 0 else (sect, tile - 1)
        return pltpu.make_async_remote_copy(
            src_ref=send,
            dst_ref=recv,
            send_sem=sems.at[0],
            recv_sem=sems.at[1],
            device_id=to,
            device_id_type=MESH,
        )

    def for_each_side(act):
        for number, sends, receives in ((0, has_south, has_north), (1, has_north, has_south)):
            act(number, sends, receives)

    def exchange(make):
        def act(number, sends, receives):
            @pl.when(sends)
            def _():
                make(number).start()

        for_each_side(act)

    def settle(make, sent, received):
        def act(number, sends, receives):
            if sent:

                @pl.when(sends)
                def _():
                    make(number).wait_send()

            if received:

                @pl.when(receives)
                def _():
                    make(number).wait_recv()

        for_each_side(act)

    def halo(step, group):
        def make(number):
            return neighbour_copy(
                halo_send.at[step, number, group],
                halo_recv.at[step, number, group],
                halo_sems.at[step, group, number],
                number,
            )

        return make

    def scale(step, group):
        def make(number):
            return neighbour_copy(
                scale_send.at[step, number, group],
                scale_recv.at[step, number, group],
                scale_sems.at[step, group, number],
                number,
            )

        return make

    half = columns // 2
    quarter = columns // 4

    def send_halo(step, group):
        part = pl.ds(8 * group, 8)
        for number in range(2):
            chunks = [halo_stage[number, part, pl.ds(q * quarter, quarter)] for q in range(4)]
            most = functools.reduce(jnp.maximum, [jnp.abs(chunk) for chunk in chunks])
            most = functools.reduce(
                jnp.maximum, [most[:, k * LANES : (k + 1) * LANES] for k in range(quarter // LANES)]
            )
            most = jnp.maximum(most, 1e-33)
            scale_send[step, number, group] = most * (1.0 / 32767.0)
            factor = jnp.concatenate([32767.0 / most] * (quarter // LANES), axis=1)
            for q in range(2):
                both = jnp.concatenate([chunks[q] * factor, chunks[q + 2] * factor], axis=0)
                halo_send[step, number, group, :, pl.ds(q * quarter, quarter)] = (
                    jnp.round(both).astype(jnp.int32).astype(jnp.int16)
                )
        exchange(scale(step, group))
        exchange(halo(step, group))

    def take_halo(step, group):
        settle(scale(step, group), False, True)
        settle(halo(step, group), False, True)
        part = pl.ds(8 * group, 8)
        for number in range(2):
            factor = jnp.concatenate([scale_recv[step, number, group]] * (quarter // LANES), axis=1)
            for q in range(2):
                both = halo_recv[step, number, group, :, pl.ds(q * quarter, quarter)].astype(jnp.int32).astype(F32)
                halo_rows[number, part, pl.ds(q * quarter, quarter)] = both[0:8] * factor
                halo_rows[number, part, pl.ds(half + q * quarter, quarter)] = both[8:16] * factor

    def edge(number):
        return neighbour_copy(edge_send.at[number], edge_recv.at[number], edge_sems.at[number], number)

    def side(number):
        return neighbour_copy(side_send.at[number], side_recv.at[number], side_sems.at[number], number)

    loads[6].wait()

    group_levels = ((1, 7), (8, 8))
    halo_stage[:, 0:1, :] = jnp.zeros((2, 1, columns), F32)
    for group in range(2):

        def rows_out(level):
            halo_stage[0, pl.ds(level, 1), :] = field_a[level, 15:16, :]
            halo_stage[1, pl.ds(level, 1), :] = field_a[level, 0:1, :]

        over_levels(*group_levels[group], rows_out)
        send_halo(0, group)

    loads[7].wait()
    loads[8].wait()
    loads[9].wait()
    wet_mask[...] = jnp.where(is_ocean, mask_int[...].astype(F32), 1.0)

    for number, row in ((0, 14), (1, 0)):
        pair = slice(row, row + 2)
        packed = jnp.concatenate(
            [
                winds[0, 0][pair].astype(F32),
                winds[1, 0][pair].astype(F32),
                mixing[0][pair].astype(F32),
                wet_mask[row : row + 2, :],
            ],
            axis=0,
        )
        side_send[number] = jnp.concatenate([packed[:, :half], packed[:, half:]], axis=0).astype(BF16)
    exchange(side)

    def coef_level(wet_ref, level):
        for start, size in column_chunks(columns, 7):
            cols = pl.ds(start, size)
            parts = coefficients(
                winds[0, level, :, cols].astype(F32),
                winds[1, level, :, cols].astype(F32),
                mixing[level, :, cols].astype(F32),
                None if wet_ref is None else wet_ref[:, cols],
                0 if start == 0 else None,
                size - 1 if start + size == columns else None,
            )
            for i, part in enumerate(parts):
                coef[i, level, :, cols] = part

    for here, wet_ref in ((is_atm, None), (is_ocean, wet_mask)):

        @pl.when(here)
        def _(wet_ref=wet_ref):
            over_levels(0, levels, functools.partial(coef_level, wet_ref), 2)

    @pl.when(is_ocean)
    def _():
        pltpu.make_async_copy(down_recv, down_recv, remap_sem.at[1]).wait()
        count = ocean_sect * tiles * 8
        arrived = down_recv[...]
        codes = arrived.astype(jnp.int32)
        targets = codes >> 10
        sources = codes & (CODE - 1)
        place_block = block_of(lanes_i((blocks, LANES), 0)) + 1
        onehots = []
        for q in range(count // LANES):
            ids = jnp.sum(targets[q * 16 : (q + 1) * 16, 4:5, :], axis=0)
            onehots.append(jnp.where(place_block == ids, 1.0, 0.0).astype(BF16))
        flux = jnp.dot(
            jnp.concatenate(onehots, axis=1),
            arrived.reshape(count, LANES).astype(BF16),
            preferred_element_type=F32,
        )
        for k in range(col_tiles):
            cols = pl.ds(k * LANES, LANES)
            wet = wet_mask[:, cols]
            warm = field_a[0, :, cols] + flux[k * rows : (k + 1) * rows] * wet
            zero_a[8:24, cols] = warm
            sst[k * rows : (k + 1) * rows, :] = (warm * wet).astype(BF16)
        sst[blocks:blocks_pad, :] = jnp.zeros((blocks_pad - blocks, LANES), BF16)
        asked = sources.reshape(count, LANES)
        gathers = [
            jnp.where(asked == block_of(lanes_i((count, LANES), 1) + q * LANES), 1.0, 0.0).astype(BF16)
            for q in range(blocks_pad // LANES)
        ]
        up_send[...] = jnp.dot(jnp.concatenate(gathers, axis=1), sst[...], preferred_element_type=F32).reshape(
            up_send.shape
        )

        def one(i, carry):
            t = lax.rem(tile + i, tiles)
            for s in range(ocean_sect):
                pltpu.make_async_remote_copy(
                    src_ref=up_send.at[s * tiles + t],
                    dst_ref=up_recv.at[tile],
                    send_sem=remap_sem.at[2],
                    recv_sem=remap_sem.at[3],
                    device_id=(s, t),
                    device_id_type=MESH,
                ).start()
            return carry

        lax.fori_loop(0, tiles, one, 0)

    def send_edges():
        for start, size in column_chunks(columns, 7):
            cols = pl.ds(start, size)
            edge_send[0, :, cols] = zero_a[20:24, cols]
            edge_send[1, :, cols] = zero_a[8:12, cols]
        exchange(edge)

    @pl.when(is_ocean)
    def _():
        send_edges()

    fields = (field_a, field_b, field_a, field_b)

    def run_group(step, group):
        src, dst = fields[step], fields[step + 1]
        take_halo(step, group)
        last = step == SUBSTEPS - 1

        def keep_rows(level):
            def keep(upper, lower, start, size):
                cols = pl.ds(start, size)
                halo_stage[0, pl.ds(level, 1), cols] = lower[7:8]
                halo_stage[1, pl.ds(level, 1), cols] = upper[0:1]

            return keep

        def one(level):
            substep_level(src, dst, coef, halo_rows, level, None if last else keep_rows(level))

        over_levels(*group_levels[group], one)
        if not last:
            send_halo(step + 1, group)

    run_group(0, 0)
    run_group(0, 1)

    loads[10].wait()

    @pl.when(is_atm)
    def _():
        pltpu.make_async_copy(up_recv, up_recv, remap_sem.at[3]).wait()

        def some(i, carry):
            for j in range(8):
                d = i * 8 + j
                lhs_all[d] = remap(up_recv, matrix_u, 4, d)
            return carry

        lax.fori_loop(0, tiles // 8, some, 0)
        returned = lhs_all[...].reshape(8 * tiles, LANES)
        high = returned.astype(BF16)
        rest = returned - high.astype(F32)
        middle = rest.astype(BF16)
        low = (rest - middle.astype(F32)).astype(BF16)
        onehot = onehot_up[...]
        total = jnp.dot(onehot, high, preferred_element_type=F32)
        total = total + jnp.dot(onehot, middle, preferred_element_type=F32)
        total = total + jnp.dot(onehot, low, preferred_element_type=F32)
        for k in range(col_tiles):
            cols = pl.ds(k * LANES, LANES)
            zero_a[8:24, cols] = field_a[0, :, cols] + 0.5 * total[k * rows : (k + 1) * rows]
        send_edges()

    run_group(1, 0)
    run_group(1, 1)

    settle(side, False, True)
    for start, size in column_chunks(columns, 7):
        cols = pl.ds(start, size)
        row = lanes_i((8, size), 0)
        for number, base, shifts, valid in ((0, 0, (6, 4, 2, 0), row >= 6), (1, 24, (0, 6, 4, 2), row < 2)):
            fold = pl.ds(start % half, size)
            packed = side_recv[number, :, fold].astype(F32)[8 * (start // half) : 8 * (start // half) + 8]
            u, v, k, wet = [pltpu.roll(packed, shift, 0) if shift else packed for shift in shifts]
            parts = coefficients(
                u,
                v,
                k,
                wet,
                0 if start == 0 else None,
                size - 1 if start + size == columns else None,
            )
            for i, part in enumerate(parts):
                coef_zero[i, base : base + 8, cols] = jnp.where(valid, part, 0.0)
    settle(edge, False, True)
    for start, size in column_chunks(columns, 7):
        cols = pl.ds(start, size)
        blank = jnp.zeros((4, size), F32)
        zero_a[0:8, cols] = jnp.concatenate([blank, edge_recv[0, :, cols]], axis=0)
        zero_a[24:32, cols] = jnp.concatenate([edge_recv[1, :, cols], blank], axis=0)

    def surface(src, dst, first, count):
        for start, size in column_chunks(columns, 7):
            cols = pl.ds(start, size)
            row = lanes_i((8, size), 0)
            before = pl.ds((start - LANES) % columns, LANES)
            after = pl.ds((start + size) % columns, LANES)
            for g in range(first, first + count):
                here = pl.ds(8 * g, 8)
                x = src[here, cols]
                down = pltpu.roll(x, 1, 0)
                up = pltpu.roll(x, 7, 0)
                if g > 0:
                    down = jnp.where(row == 0, pltpu.roll(src[8 * g - 8 : 8 * g, cols], 1, 0), down)
                if g < 3:
                    up = jnp.where(row == 7, pltpu.roll(src[8 * g + 8 : 8 * g + 16, cols], 7, 0), up)
                east, west = shifted_columns(x, src[here, before], src[here, after])
                if g in (1, 2):
                    inner = pl.ds(8 * g - 8, 8)
                    c = [coef[i, 0, inner, cols] for i in range(5)]
                else:
                    c = [coef_zero[i, here, cols] for i in range(5)]
                new = c[0] * x + c[1] * east + c[2] * west + c[3] * down + c[4] * up
                if dst is None:
                    field_b[0, inner, cols] = new
                else:
                    dst[here, cols] = new

    surface(zero_a, zero_b, 0, 4)
    surface(zero_b, zero_a, 0, 4)
    surface(zero_a, None, 1, 2)

    run_group(2, 0)
    run_group(2, 1)

    @pl.when(is_atm)
    def _():
        pltpu.make_async_copy(down_send, down_send, remap_sem.at[0]).wait()

    @pl.when(is_ocean)
    def _():
        pltpu.make_async_copy(up_send, up_send, remap_sem.at[2]).wait()

    for step in range(SUBSTEPS):
        for group in range(2):
            settle(scale(step, group), True, False)
            settle(halo(step, group), True, False)
    settle(edge, True, False)
    settle(side, True, False)


def write_out(result, out, sem):
    copy = pltpu.make_async_copy(result, out, sem)
    copy.start()
    copy.wait()


def per_device(
    sections,
    tracer_values,
    courant_numbers,
    diffusion_numbers,
    water_indicator,
    downward_lane_pairs,
    downward_lane_number,
    downward_patch_matrix,
    upward_lane_pairs,
    upward_lane_number,
    upward_patch_matrix,
):
    tracer = tracer_values[0]
    levels, rows, columns = tracer.shape
    tiles, slots = downward_lane_pairs.shape[-2:]
    stacked = (SUBSTEPS, 2, levels // 8)
    partners = (sections - 1) * tiles
    blocks = rows * columns // LANES
    vmem = pltpu.VMEM
    dma = pltpu.SemaphoreType.DMA
    whole = pl.BlockSpec(memory_space=pl.ANY)
    operands = (
        tracer,
        courant_numbers[:, 0],
        diffusion_numbers[0],
        water_indicator,
        jnp.swapaxes(downward_lane_pairs[0, 0], 1, 2),
        downward_lane_number[0],
        downward_patch_matrix[0, 0],
        jnp.swapaxes(upward_lane_pairs[0, 0], 1, 2),
        upward_lane_number[0],
        upward_patch_matrix[0, 0],
    )
    result = pl.pallas_call(
        functools.partial(kernel_body, sections, tiles),
        out_shape=pltpu.VMEM(tracer.shape, F32),
        in_specs=[whole] * len(operands),
        out_specs=pl.BlockSpec(memory_space=pltpu.VMEM),
        scratch_shapes=[
            vmem((levels, rows, columns), F32),
            vmem((2, levels, rows, columns), BF16),
            vmem((levels, rows, columns), BF16),
            vmem((5, levels, rows, columns), F32),
            vmem((rows, columns), jnp.int32),
            vmem((rows, columns), F32),
            vmem((2, slots, tiles), jnp.int32),
            vmem((1, tiles), jnp.int32),
            vmem((tiles, slots, LANES, LANES), BF16),
            vmem((2, slots, tiles), jnp.int32),
            vmem((1, tiles), jnp.int32),
            vmem((tiles, slots, LANES, LANES), BF16),
            vmem((tiles, 8, LANES), F32),
            vmem((partners, 8, LANES), F32),
            vmem((partners, 8, LANES), F32),
            vmem((tiles, 8, LANES), F32),
            vmem((tiles, 8, LANES), F32),
            vmem((blocks, 8 * tiles), BF16),
            vmem((512, LANES), BF16),
            vmem((2, levels, columns), F32),
            vmem((2, levels, columns), F32),
            vmem((*stacked, 16, columns // 2), jnp.int16),
            vmem((*stacked, 16, columns // 2), jnp.int16),
            vmem((*stacked, 8, LANES), F32),
            vmem((*stacked, 8, LANES), F32),
            vmem((2, 4, columns), F32),
            vmem((2, 4, columns), F32),
            vmem((2, 16, columns // 2), BF16),
            vmem((2, 16, columns // 2), BF16),
            vmem((32, columns), F32),
            vmem((32, columns), F32),
            vmem((5, 32, columns), F32),
            dma((11,)),
            dma((4,)),
            dma((SUBSTEPS, 2, 2, 2)),
            dma((SUBSTEPS, 2, 2, 2)),
            dma((2, 2)),
            dma((2, 2)),
        ],
        compiler_params=pltpu.CompilerParams(
            collective_id=0, has_side_effects=True, vmem_limit_bytes=54 * 2**20
        ),
    )(*operands)
    result = pl.pallas_call(
        write_out,
        out_shape=jax.ShapeDtypeStruct(tracer.shape, F32),
        in_specs=[pl.BlockSpec(memory_space=pltpu.VMEM)],
        out_specs=whole,
        scratch_shapes=[dma(())],
        compiler_params=pltpu.CompilerParams(vmem_limit_bytes=2**20),
    )(result)
    return result[None]


def solution(mesh):
    placed = (
        P("sect", None, "tile", None),
        P(None, "sect", None, "tile", None),
        P("sect", None, "tile", None),
        P("tile", None),
        P("sect", "tile", None, None, None),
        P("sect", "tile", None),
        P("sect", "tile", None, None, None, None),
        P("sect", "tile", None, None, None),
        P("sect", "tile", None),
        P("sect", "tile", None, None, None, None),
    )
    return jax.shard_map(
        functools.partial(per_device, mesh.shape["sect"]),
        mesh=mesh,
        in_specs=placed,
        out_specs=P("sect", None, "tile", None),
        check_vma=False,
    )
```
